32 devices in a mesh: dp: 4 (over y, x), ctx: 8 (over z, core).
Axes of the slice: x: 2, y: 2, z: 4, core: 2. Of those that a mesh axis runs over, the one named last changes fastest.
Arguments:
- tokens: bfloat16 [4, 4096, 1024], P('dp', 'ctx'), may hold values from -900 to 900
- grad_output: bfloat16 [4, 4096, 1024], P('dp', 'ctx'), may hold values from -6 to 6
- session_ids: int32 [4], P('dp'), may hold values from 0 to 63
- session_table: bfloat16 [64, 1024], replicated, may hold values from -6 to 6
- norm_gain: bfloat16 [1024], P('dp'), may hold values from 0.099609375 to 1.8984375
- input_weight: bfloat16 [1024, 2304], P('dp'), may hold values from -0.1875 to 0.1875
- step_weight: bfloat16 [1024, 16], P('dp'), may hold values from -1 to 1
- head_params: float32 [3, 16], replicated, may hold values from -9 to 4
- gate_gain: bfloat16 [1024], P('dp'), may hold values from 0.099609375 to 1.8984375
- output_weight: bfloat16 [1024, 1024], P('dp'), may hold values from -0.1875 to 0.1875
Outputs:
- tokens_grad: bfloat16 [4, 4096, 1024], P('dp', 'ctx')
- norm_grad: float32 [1024], P(('dp', 'ctx'))
- input_grad: float32 [1024, 2304], P(('dp', 'ctx'))
- step_grad: float32 [1024, 16], P(('dp', 'ctx'))
- head_grad: float32 [3, 16], replicated
- gate_grad: float32 [1024], P(('dp', 'ctx'))
- output_grad: float32 [1024, 1024], P(('dp', 'ctx'))
- table_grad: float32 [64, 1024], P(None, ('dp', 'ctx'))
The draws below stay inside these ranges and needn't reach their ends.
All inputs are finite; a program needn't handle non-finite values.
Results may differ from the reference program's by a relative error of at most 0.005.
The reference program's roundings to bfloat16 on the way (of `norm_act`, `mixed_out` and `grad_proj`) count: a program that leaves them out, or rounds other values in their place, can miss the bound.
Values may be sent and summed in bfloat16 or wider, within the bound.
A program may use at most 128 MiB of HBM per device.

```python
import math
import jax
import jax.numpy as jnp
from jax import lax

D = 1024
HEADS = 16
HEAD = 64
STATE = 128
SESSIONS = 64
BINS_DEV = 512
INNER = 1024
PROJ = 2304
BATCH = 4
LENGTH = 4096


def volley_bearing(key):
    return jnp.clip(jax.random.normal(jax.random.fold_in(key, 7), (D,), jnp.float32), -4.0, 4.0)


def draw_tokens(key, part):
    derivative_trial_arrow = volley_bearing(key)
    keys = jax.random.split(jax.random.fold_in(key, 11), 5)
    gaussian_disturbance = jnp.clip(jax.random.normal(keys[0], (BATCH, LENGTH, D), jnp.float32), -4.0, 4.0)
    lateral_coefficient = jnp.exp(jax.random.uniform(keys[1], (BATCH, LENGTH, 1), jnp.float32, 0.0, math.log(10.0)))
    upright_coefficient = jnp.exp(jax.random.uniform(keys[2], (1, 1, D), jnp.float32, 0.0, math.log(10.0)))
    finite_step_length = jax.random.uniform(keys[3], (BATCH, LENGTH // 256, 1), jnp.float32, 0.0, 0.5)
    finite_step_length = jnp.repeat(finite_step_length, 256, axis=1)
    spots = jax.random.randint(keys[4], (BATCH, 3), 0, LENGTH)
    concordant_cases = jnp.arange(LENGTH)[None, :, None] == spots[:, None, :]
    neuron_discharge_train = jnp.any(concordant_cases, axis=-1).astype(jnp.float32)[:, :, None]
    quantity_items = lateral_coefficient * (upright_coefficient * gaussian_disturbance + (finite_step_length + 10.0 * neuron_discharge_train) * derivative_trial_arrow[None, None, :])
    return quantity_items.astype(jnp.bfloat16)


def draw_step_weight(key, part):
    derivative_trial_arrow = volley_bearing(key)
    gaussian_disturbance = jnp.clip(jax.random.normal(jax.random.fold_in(key, 13), (D, HEADS), jnp.float32), -4.0, 4.0)
    quantity_items = gaussian_disturbance / math.sqrt(D) + derivative_trial_arrow[:, None] * (10.0 / D)
    return quantity_items.astype(jnp.bfloat16)


def draw_head_params(key, part):
    keys = jax.random.split(jax.random.fold_in(key, 17), 5)
    bias = jax.random.uniform(keys[0], (HEADS,), jnp.float32, -8.5, -7.5)
    slow = math.log(1.0 / (LENGTH * 0.001))
    fast = math.log(1.0 / (40.0 * 0.001))
    lower = jax.random.uniform(keys[1], (HEADS,), jnp.float32, slow, slow + 0.7)
    upper = jax.random.uniform(keys[2], (HEADS,), jnp.float32, slow + 0.7, fast)
    picked = jax.random.bernoulli(keys[3], 0.5, (HEADS,))
    log_rate = jnp.where(picked, lower, upper)
    skip = jax.random.uniform(keys[4], (HEADS,), jnp.float32, 0.5, 1.5)
    return jnp.stack([bias, log_rate, skip]).astype(jnp.float32)


def place_ends(entries, stream_key, smallest, largest):
    extent = entries.shape
    spot = [jax.random.randint(jax.random.fold_in(stream_key, axis), (), 0, extent[axis]) for axis in range(len(extent))]
    entries = entries.at[tuple(spot)].set(smallest)
    longest = extent.index(max(extent))
    spot[longest] = (spot[longest] + 1) % extent[longest]
    return entries.at[tuple(spot)].set(largest)


def block_scale(stream_key, extent, shards, least, high):
    factor_of = 1.0
    for dim, shards_of in shards:
        steps = jax.random.uniform(jax.random.fold_in(jax.random.fold_in(stream_key, 6), dim), (shards_of,), jnp.float32, least / len(shards), high / len(shards))
        factor_of = factor_of * jnp.repeat(jnp.exp(steps), extent[dim] // shards_of).reshape((-1,) + (1,) * (len(extent) - 1 - dim))
    return factor_of


def centred(own_key, extent, scale, bound, shards=(), held_as=jnp.bfloat16):
    values = scale * jax.random.normal(own_key, extent, jnp.float32)
    if shards:
        values = values * block_scale(own_key, extent, shards, -0.22, 0.18)
    return jnp.clip(values, -bound, bound).astype(held_as)


def setup_inputs(seed: int = 0) -> dict:
    key_of = jax.random.split(jax.random.key(seed), 11)
    tokens = draw_tokens(jax.random.fold_in(key_of[10], 71), 0)
    grad_output = centred(key_of[1], (BATCH, LENGTH, D), 1.0, 6.0, ((0, 4), (1, 8)))
    session_ids = place_ends(jax.random.randint(key_of[2], (BATCH,), 0, SESSIONS), jax.random.fold_in(key_of[2], 1), 0, SESSIONS - 1).astype(jnp.int32)
    session_table = centred(key_of[3], (SESSIONS, D), 1.0, 6.0)
    norm_gain = jnp.clip(1.0 + 0.18 * jax.random.normal(key_of[4], (D,), jnp.float32), 0.099609375, 1.8984375).astype(jnp.bfloat16)
    input_weight = centred(key_of[5], (D, PROJ), D ** -0.5, 0.1875, ((0, 4),))
    step_weight = draw_step_weight(jax.random.fold_in(key_of[10], 71), 0)
    head_params = draw_head_params(jax.random.fold_in(key_of[10], 71), 0)
    gate_gain = jnp.clip(1.0 + 0.18 * jax.random.normal(key_of[8], (INNER,), jnp.float32), 0.099609375, 1.8984375).astype(jnp.bfloat16)
    output_weight = centred(key_of[9], (INNER, D), INNER ** -0.5, 0.1875, ((0, 4),))
    return {"tokens": tokens, "grad_output": grad_output, "session_ids": session_ids, "session_table": session_table, "norm_gain": norm_gain, "input_weight": input_weight, "step_weight": step_weight, "head_params": head_params, "gate_gain": gate_gain, "output_weight": output_weight}


epsilon = 1e-05

def normalize(quantity_items):
    factor = lax.rsqrt(lax.optimization_barrier(jnp.mean(quantity_items * quantity_items, axis=-1, keepdims=True)) + epsilon)
    return (quantity_items * factor, factor)

def block_prep(value_raw, step_raw, head_params):
    length = value_raw.shape[0]
    num_heads = step_raw.shape[1]
    activated = jax.nn.silu(value_raw)
    step_size = jax.nn.softplus(step_raw + head_params[0][None, :])
    log_rate = -jnp.exp(head_params[1])[None, :] * step_size
    log_decay = jnp.cumsum(log_rate, axis=0)
    scaled_in = step_size[:, :, None] * activated.reshape(length, num_heads, -1)
    return (activated, log_decay, scaled_in)

def state_block(value_raw, in_map, out_map, step_raw, head_params, state_in):
    length = value_raw.shape[0]
    num_heads = step_raw.shape[1]
    activated, log_decay, scaled_in = block_prep(value_raw, step_raw, head_params)
    positions = jnp.arange(length)
    causal = positions[:, None] >= positions[None, :]
    decay_log = log_decay.T
    decay_gap = jnp.where(causal[None], decay_log[:, :, None] - decay_log[:, None, :], 0.0)
    mask_decay = jnp.where(causal[None], jnp.exp(decay_gap), 0.0)
    scores = jnp.dot(out_map, in_map.T, precision=lax.Precision.HIGHEST)
    weighted = mask_decay * scores[None]
    result = jnp.einsum('hqk,khp->qhp', weighted, scaled_in, precision=lax.Precision.HIGHEST)
    carried = jnp.einsum('qn,hpn->qhp', out_map, state_in, precision=lax.Precision.HIGHEST)
    result = result + jnp.exp(log_decay)[:, :, None] * carried
    result = result + head_params[2][None, :, None] * activated.reshape(length, num_heads, -1)
    decay_tail = jnp.exp(log_decay[-1][None, :] - log_decay)
    fresh = jnp.einsum('kh,khp,kn->hpn', decay_tail, scaled_in, in_map, precision=lax.Precision.HIGHEST)
    state_out = jnp.exp(log_decay[-1])[:, None, None] * state_in + fresh
    return (result.reshape(length, -1), state_out)

def sequence_core(value_raw, in_map, out_map, step_raw, head_params):
    blocks = value_raw.shape[0] // BINS_DEV

    def advance(carry, pieces):
        result, state_out = state_block(pieces[0], pieces[1], pieces[2], pieces[3], head_params, carry)
        return (state_out, result)
    pieces = (value_raw.reshape(blocks, BINS_DEV, -1), in_map.reshape(blocks, BINS_DEV, -1), out_map.reshape(blocks, BINS_DEV, -1), step_raw.reshape(blocks, BINS_DEV, -1))
    start = jnp.zeros((HEADS, HEAD, STATE), jnp.float32)
    ending, results = lax.scan(jax.checkpoint(advance), start, pieces)
    return results.reshape(value_raw.shape[0], -1)

def one_sequence(tokens_row, grad_row, table_row, norm_gain, input_weight, step_weight, head_params, gate_gain, output_weight):
    norm_wide = norm_gain.astype(jnp.float32)
    gate_wide = gate_gain.astype(jnp.float32)
    layer_in = tokens_row.astype(jnp.float32) + table_row.astype(jnp.float32)[None, :]
    normed, in_scale = normalize(layer_in)
    norm_act = (normed * norm_wide[None, :]).astype(jnp.bfloat16)
    projected = jnp.dot(norm_act, input_weight, preferred_element_type=jnp.float32)
    step_raw = jnp.dot(norm_act, step_weight, preferred_element_type=jnp.float32)
    gate_pre = projected[:, :INNER]
    value_raw = projected[:, INNER:2 * INNER]
    in_map = projected[:, 2 * INNER:2 * INNER + STATE]
    out_map = projected[:, 2 * INNER + STATE:]
    ssd_out, core_back = jax.vjp(sequence_core, value_raw, in_map, out_map, step_raw, head_params)
    gated = ssd_out * jax.nn.silu(gate_pre)
    gated_norm, gate_scale = normalize(gated)
    mixed_out = (gated_norm * gate_wide[None, :]).astype(jnp.bfloat16)
    grad_mixed = jnp.dot(grad_row, output_weight.T, preferred_element_type=jnp.float32)
    term_output = jnp.dot(mixed_out.T, grad_row, preferred_element_type=jnp.float32)
    term_gate = lax.optimization_barrier(jnp.sum(grad_mixed * gated_norm, axis=0))
    grad_gnorm = grad_mixed * gate_wide[None, :]
    grad_gated = gate_scale * (grad_gnorm - gated_norm * lax.optimization_barrier(jnp.mean(grad_gnorm * gated_norm, axis=-1, keepdims=True)))
    gate_sig = jax.nn.sigmoid(gate_pre)
    grad_ssd = grad_gated * jax.nn.silu(gate_pre)
    grad_gate = grad_gated * ssd_out * gate_sig * (1.0 + gate_pre * (1.0 - gate_sig))
    grad_value, grad_in_map, grad_out_map, grad_step_raw, grad_heads = core_back(grad_ssd)
    grad_proj = jnp.concatenate([grad_gate, grad_value, grad_in_map, grad_out_map], axis=1).astype(jnp.bfloat16)
    grad_step_low = grad_step_raw.astype(jnp.bfloat16)
    grad_act = jnp.dot(grad_proj, input_weight.T, preferred_element_type=jnp.float32)
    grad_act = grad_act + jnp.dot(grad_step_low, step_weight.T, preferred_element_type=jnp.float32)
    term_input = jnp.dot(norm_act.T, grad_proj, preferred_element_type=jnp.float32)
    term_step = jnp.dot(norm_act.T, grad_step_low, preferred_element_type=jnp.float32)
    term_norm = lax.optimization_barrier(jnp.sum(grad_act * normed, axis=0))
    grad_normed = grad_act * norm_wide[None, :]
    grad_input = in_scale * (grad_normed - normed * lax.optimization_barrier(jnp.mean(grad_normed * normed, axis=-1, keepdims=True)))
    terms = (term_norm, term_input, term_step, grad_heads, term_gate, term_output, lax.optimization_barrier(jnp.sum(grad_input, axis=0)))
    return (grad_input.astype(jnp.bfloat16), terms)

def reference(tokens, grad_output, session_ids, session_table, norm_gain, input_weight, step_weight, head_params, gate_gain, output_weight):
    table_rows = session_table[session_ids]

    def per_sequence(pieces):
        return one_sequence(pieces[0], pieces[1], pieces[2], norm_gain, input_weight, step_weight, head_params, gate_gain, output_weight)
    tokens_grad, terms = lax.map(per_sequence, (tokens, grad_output, table_rows))
    grad_scale = 1.0 / math.sqrt(BATCH * LENGTH)
    totals = [lax.optimization_barrier(jnp.sum(term, axis=0)) * grad_scale for term in terms[:6]]
    session_hot = (session_ids[:, None] == jnp.arange(SESSIONS)[None, :]).astype(jnp.float32)
    table_grad = jnp.dot(session_hot.T, terms[6], precision=lax.Precision.HIGHEST) * grad_scale
    return (tokens_grad, totals[0], totals[1], totals[2], totals[3], totals[4], totals[5], table_grad)
```

```python
import functools
import math

import jax
import jax.numpy as jnp
from jax import lax
from jax.experimental import pallas as pl
from jax.experimental.pallas import tpu as pltpu
from jax.sharding import PartitionSpec as P

epsilon = 1e-05
CHUNK = 128
PAIR = 128
F32 = jnp.float32
BF16 = jnp.bfloat16
HIGHEST = lax.Precision.HIGHEST
HIGH = lax.Precision.HIGH
NN = (((1,), (0,)), ((), ()))
NT = (((1,), (1,)), ((), ()))
TN = (((0,), (0,)), ((), ()))


def split(value):
    high = value.astype(BF16)
    return (high, (value - high.astype(F32)).astype(BF16))


def dot3(left, right, dims):
    one = functools.partial(lax.dot_general, dimension_numbers=dims, preferred_element_type=F32)
    return one(left[0], right[0]) + (one(left[0], right[1]) + one(left[1], right[0]))


def chunk_rows(c):
    return slice(c * CHUNK, (c + 1) * CHUNK)


def forward_kernel(v_ref, dt_ref, log_ref, row_ref, in_ref, in_t_ref, out_ref, y_ref, scores):
    chunks = v_ref.shape[0] // CHUNK

    @pl.when(pl.program_id(0) == 0)
    def _():
        for c in range(chunks):
            rows = chunk_rows(c)
            scores[c] = dot3(split(out_ref[rows, :]), split(in_ref[rows, :]), NT)

    lane = lax.broadcasted_iota(jnp.int32, (CHUNK, PAIR), 1)
    later = lax.broadcasted_iota(jnp.int32, (CHUNK, CHUNK), 0)
    causal = later >= lax.broadcasted_iota(jnp.int32, (CHUNK, CHUNK), 1)
    state = None
    for c in range(chunks):
        rows = chunk_rows(c)
        v = v_ref[rows, :]
        scaled = dt_ref[rows, :] * (v * jax.nn.sigmoid(v))
        log = log_ref[rows, :]
        result = None
        for h in range(2):
            column = jnp.broadcast_to(log[:, h * 64 : h * 64 + 1], (CHUNK, CHUNK))
            gap = column - row_ref[0, h : h + 1, rows]
            weights = jnp.where(causal, jnp.exp(jnp.where(causal, gap, 0.0)), 0.0) * scores[c]
            mine = jnp.where((lane < 64) == (h == 0), scaled, 0.0)
            part = dot3(split(weights), split(mine), NN)
            result = part if result is None else result + part
        if state is not None:
            result = result + jnp.exp(log) * dot3(split(out_ref[rows, :]), split(state), NN)
        y_ref[rows, :] = result
        if c + 1 < chunks:
            last = log[CHUNK - 1 : CHUNK, :]
            fresh = dot3(split(in_t_ref[:, rows]), split(jnp.exp(last - log) * scaled), NN)
            state = fresh if state is None else jnp.exp(last) * state + fresh


def backward_kernel(
    v_ref,
    dt_ref,
    log_ref,
    row_ref,
    in_ref,
    in_t_ref,
    out_ref,
    out_t_ref,
    grad_ref,
    state_ref,
    dx_ref,
    din_ref,
    dout_ref,
    scores,
    dscores,
):
    chunks = v_ref.shape[0] // CHUNK
    step = pl.program_id(0)

    @pl.when(step == 0)
    def _():
        dscores[...] = jnp.zeros_like(dscores)
        din_ref[...] = jnp.zeros_like(din_ref)
        dout_ref[...] = jnp.zeros_like(dout_ref)
        for c in range(chunks):
            rows = chunk_rows(c)
            scores[c] = dot3(split(in_ref[rows, :]), split(out_ref[rows, :]), NT)

    lane = lax.broadcasted_iota(jnp.int32, (CHUNK, PAIR), 1)
    earlier = lax.broadcasted_iota(jnp.int32, (CHUNK, CHUNK), 0)
    causal = earlier <= lax.broadcasted_iota(jnp.int32, (CHUNK, CHUNK), 1)
    states = [state_ref[...]]
    inputs = []
    for c in range(chunks):
        rows = chunk_rows(c)
        v = v_ref[rows, :]
        scaled = dt_ref[rows, :] * (v * jax.nn.sigmoid(v))
        log = log_ref[rows, :]
        last = log[CHUNK - 1 : CHUNK, :]
        tail = jnp.exp(last - log)
        tailed = split(tail * scaled)
        inputs.append((scaled, log, last, tail, tailed))
        if c + 1 < chunks:
            fresh = dot3(split(in_t_ref[:, rows]), tailed, NN)
            states.append(jnp.exp(last) * states[c] + fresh)
    adjoint = None
    for c in reversed(range(chunks)):
        rows = chunk_rows(c)
        scaled, log, last, tail, tailed = inputs[c]
        grad = grad_ref[rows, :]
        grad_split = split(grad)
        decayed = split(jnp.exp(log) * grad)
        dout_ref[rows, :] += dot3(decayed, split(states[c]), NT)
        dx = None
        if adjoint is not None:
            adjoint_split = split(adjoint)
            dx = tail * dot3(split(in_ref[rows, :]), adjoint_split, NN)
            din_ref[rows, :] += dot3(tailed, adjoint_split, NT)
        total = dscores[c]
        for h in range(2):
            own = (lane < 64) == (h == 0)
            column = jnp.broadcast_to(log[:, h * 64 : h * 64 + 1], (CHUNK, CHUNK))
            gap = row_ref[0, h : h + 1, rows] - column
            decay = jnp.where(causal, jnp.exp(jnp.where(causal, gap, 0.0)), 0.0)
            mine = split(jnp.where(own, grad, 0.0))
            part = dot3(split(decay * scores[c]), mine, NN)
            dx = part if dx is None else dx + part
            total = total + decay * dot3(split(scaled), mine, NT)
        dscores[c] = total
        dx_ref[rows, :] = dx
        if c > 0:
            fresh = dot3(split(out_t_ref[:, rows]), decayed, NN)
            adjoint = fresh if adjoint is None else jnp.exp(last) * adjoint + fresh

    @pl.when(step == pl.num_programs(0) - 1)
    def _():
        for c in range(chunks):
            rows = chunk_rows(c)
            total = split(dscores[c])
            din_ref[rows, :] += dot3(total, split(out_ref[rows, :]), NN)
            dout_ref[rows, :] += dot3(total, split(in_ref[rows, :]), TN)


def pair_block(bins):
    return pl.BlockSpec((bins, PAIR), lambda j: (0, j))


def whole(shape):
    return pl.BlockSpec(shape, lambda j: (0,) * len(shape))


def core_forward(v, dt, log, row, in_map, in_t, out_map):
    bins, width = v.shape
    pairs, chunks = width // PAIR, bins // CHUNK
    block = pair_block(bins)
    return pl.pallas_call(
        forward_kernel,
        grid=(pairs,),
        out_shape=jax.ShapeDtypeStruct((bins, width), F32),
        in_specs=[
            block,
            block,
            block,
            pl.BlockSpec((1, 2, bins), lambda j: (j, 0, 0)),
            whole(in_map.shape),
            whole(in_t.shape),
            whole(out_map.shape),
        ],
        out_specs=block,
        scratch_shapes=[pltpu.VMEM((chunks, CHUNK, CHUNK), F32)],
        compiler_params=pltpu.CompilerParams(vmem_limit_bytes=40 * 1024 * 1024),
        cost_estimate=pl.CostEstimate(
            flops=pairs * chunks * 36 * 128**3, bytes_accessed=16 * bins * width, transcendentals=0
        ),
        name="core_forward",
    )(v, dt, log, row, in_map, in_t, out_map)


def core_backward(v, dt, log, row, in_map, in_t, out_map, out_t, grad, state):
    bins, width = v.shape
    pairs, chunks = width // PAIR, bins // CHUNK
    block = pair_block(bins)
    return pl.pallas_call(
        backward_kernel,
        grid=(pairs,),
        out_shape=[
            jax.ShapeDtypeStruct((bins, width), F32),
            jax.ShapeDtypeStruct(in_map.shape, F32),
            jax.ShapeDtypeStruct(out_map.shape, F32),
        ],
        in_specs=[
            block,
            block,
            block,
            pl.BlockSpec((1, 2, bins), lambda j: (j, 0, 0)),
            whole(in_map.shape),
            whole(in_t.shape),
            whole(out_map.shape),
            whole(out_t.shape),
            block,
            pl.BlockSpec((state.shape[0], PAIR), lambda j: (0, j)),
        ],
        out_specs=[block, whole(in_map.shape), whole(out_map.shape)],
        scratch_shapes=[
            pltpu.VMEM((chunks, CHUNK, CHUNK), F32),
            pltpu.VMEM((chunks, CHUNK, CHUNK), F32),
        ],
        compiler_params=pltpu.CompilerParams(vmem_limit_bytes=40 * 1024 * 1024),
        cost_estimate=pl.CostEstimate(
            flops=pairs * chunks * 80 * 128**3, bytes_accessed=24 * bins * width, transcendentals=0
        ),
        name="core_backward",
    )(v, dt, log, row, in_map, in_t, out_map, out_t, grad, state)


def swap_ctx(value, bit):
    count = lax.axis_size("ctx")
    return lax.ppermute(value, "ctx", [(i, i ^ bit) for i in range(count)])


def bits_of(count):
    return [1 << b for b in range(count.bit_length() - 1)]


def dp_order(core):
    bits = bits_of(lax.axis_size("dp"))
    return bits if core == 0 else bits[::-1]


def swap_dp(value, stage):
    data_count, context_count = lax.axis_size("dp"), lax.axis_size("ctx")
    pairs = []
    for d in range(data_count):
        for c in range(context_count):
            partner = d ^ dp_order(c % 2)[stage]
            pairs.append((d * context_count + c, partner * context_count + c))
    return lax.ppermute(value, ("dp", "ctx"), pairs)


def dp_masks(core):
    first, second = dp_order(0), dp_order(1)
    return [jnp.where(core == 0, a, b) for a, b in zip(first, second)]


def pick(value, index, axis=0):
    return lax.dynamic_index_in_dim(value, index, axis, keepdims=False)


def halve(term, mine, masks, swap, wire):
    relative = [0]
    for mask in masks[::-1]:
        relative = relative + [r ^ mask for r in relative]
    term = jnp.stack([pick(term, mine ^ r) for r in relative])
    for stage in range(len(masks)):
        half = term.shape[0] // 2
        got = swap(term[half:].astype(wire), stage)
        term = term[:half] + got.astype(F32)
    return term[0]


def halve_core(term, core, wire):
    got = swap_ctx(pick(term, 1 - core, 2).astype(wire), 1)
    return pick(term, core, 2) + got.astype(F32)


def halve_dp(term, wire):
    core = lax.axis_index("ctx") % 2
    return halve(term, lax.axis_index("dp"), dp_masks(core), swap_dp, wire)


def halve_chips(term, wire):
    bits = bits_of(lax.axis_size("ctx") // 2)
    swap = lambda value, stage: swap_ctx(value, 2 * bits[stage])
    return halve(term, lax.axis_index("ctx") // 2, bits, swap, wire)


def blocks(term):
    data_count, context_count = lax.axis_size("dp"), lax.axis_size("ctx")
    rows = term.shape[0] // (data_count * context_count)
    return term.reshape((data_count, context_count // 2, 2, rows) + term.shape[1:])


def scatter_sum(term, wire):
    core = lax.axis_index("ctx") % 2
    term = halve_core(blocks(term), core, wire)
    return halve_chips(halve_dp(term, wire), wire)


def gather_rows(shard):
    data_count = lax.axis_size("dp")
    mine, core = lax.axis_index("dp"), lax.axis_index("ctx") % 2
    half = shard.shape[0] // 2
    held = lax.dynamic_slice_in_dim(shard, core * half, half, 0)[None]
    where = [mine]
    for stage, mask in enumerate(dp_masks(core)):
        held = jnp.concatenate([held, swap_dp(held, stage)])
        where = where + [w ^ mask for w in where]
    other = swap_ctx(held, 1)
    their_where = [mine]
    for mask in dp_masks(1 - core):
        their_where = their_where + [w ^ mask for w in their_where]
    full = jnp.zeros((data_count, 2) + held.shape[1:], shard.dtype)
    for i in range(data_count):
        full = lax.dynamic_update_slice(full, held[i][None, None], (where[i], core, 0, 0))
        full = lax.dynamic_update_slice(
            full, other[i][None, None], (their_where[i], 1 - core, 0, 0)
        )
    return full.reshape((-1,) + shard.shape[1:])


def carried_in(log_total, state, expand, backward):
    mine = lax.axis_index("ctx")
    core = mine % 2
    half = state.shape[0] // 2

    def is_after(bit):
        is_high = (mine & bit) != 0
        return jnp.logical_not(is_high) if backward else is_high

    partner = swap_ctx(state, 1)
    partner_log = swap_ctx(log_total, 1)
    late = is_after(1)
    late_log = jnp.where(late, log_total, partner_log)
    own_half = lax.dynamic_slice_in_dim(state, core * half, half, 0)
    partner_half = lax.dynamic_slice_in_dim(partner, core * half, half, 0)
    early_half = jnp.where(late, partner_half, own_half)
    late_half = jnp.where(late, own_half, partner_half)
    total = jnp.exp(expand(late_log)) * early_half + late_half
    total_log = log_total + partner_log
    prefix_log, prefix = jnp.zeros_like(log_total), jnp.zeros_like(total)
    for bit in bits_of(lax.axis_size("ctx"))[1:]:
        got = swap_ctx(total, bit)
        got_log = swap_ctx(total_log, bit)
        after = is_after(bit)
        prefix = jnp.where(after, jnp.exp(expand(prefix_log)) * got + prefix, prefix)
        prefix_log = jnp.where(after, prefix_log + got_log, prefix_log)
        joined_mine = jnp.exp(expand(total_log)) * got + total
        total = jnp.where(after, joined_mine, jnp.exp(expand(got_log)) * total + got)
        total_log = total_log + got_log
    other = swap_ctx(prefix, 1)
    first = jnp.where(core == 0, prefix, other)
    second = jnp.where(core == 0, other, prefix)
    whole_prefix = jnp.concatenate([first, second], axis=0)
    return jnp.where(late, jnp.exp(expand(partner_log)) * whole_prefix + partner, whole_prefix)


def fdot(left, right, dims, precision=HIGH):
    return lax.dot_general(left, right, dims, precision=precision, preferred_element_type=F32)


def per_device(
    tokens,
    grad_output,
    session_ids,
    session_table,
    norm_gain,
    input_weight,
    step_weight,
    head_params,
    gate_gain,
    output_weight,
):
    data_count, context_count = lax.axis_size("dp"), lax.axis_size("ctx")
    num_seqs, bins, model_width = tokens.shape
    assert num_seqs == 1
    width = output_weight.shape[0] * data_count
    num_heads = step_weight.shape[1]
    head_width = width // num_heads
    state_width = (input_weight.shape[1] - 2 * width) // 2
    sessions = session_table.shape[0]
    chunks = bins // CHUNK
    grad_scale = 1.0 / math.sqrt(bins * data_count * context_count)
    tokens, grad_output = tokens[0], grad_output[0]

    side = jnp.concatenate([step_weight, norm_gain[:, None], gate_gain[:, None]], axis=1)
    side_full = gather_rows(side)
    input_full = gather_rows(input_weight)
    output_full = gather_rows(output_weight)
    step_full = side_full[:, :num_heads]
    norm_full = side_full[:, num_heads].astype(F32)[None, :]
    gate_full = side_full[:, num_heads + 1].astype(F32)[None, :]

    table_row = lax.dynamic_slice_in_dim(session_table, session_ids[0], 1, 0).astype(F32)
    layer_in = tokens.astype(F32) + table_row
    in_scale = lax.rsqrt(jnp.mean(layer_in * layer_in, axis=-1, keepdims=True) + epsilon)
    normed = layer_in * in_scale
    norm_act = (normed * norm_full).astype(BF16)
    projected = fdot(norm_act, input_full, NN, None)
    step_raw = fdot(norm_act, step_full, NN, None)
    gate_pre = projected[:, :width]
    value_raw = projected[:, width : 2 * width]
    in_map = projected[:, 2 * width : 2 * width + state_width]
    out_map = projected[:, 2 * width + state_width :]
    in_t, out_t = in_map.T, out_map.T

    step_in = step_raw + head_params[0][None, :]
    step_size = jax.nn.softplus(step_in)
    rate = jnp.exp(head_params[1])[None, :]
    log_rate = -rate * step_size
    position = jnp.arange(bins)
    lower = position[:, None] >= position[None, :]
    same = (position[:, None] // CHUNK) == (position[None, :] // CHUNK)
    lower_all = lower.astype(F32)
    lower_chunk = (lower & same).astype(F32)
    log_local = fdot(lower_chunk, log_rate, NN, HIGHEST)
    log_row = fdot(log_rate, lower_chunk, (((0,), (1,)), ((), ())), HIGHEST)
    log_decay = fdot(lower_all, log_rate, NN, HIGHEST)
    log_total = jnp.sum(log_rate, axis=0)
    hot = (jnp.arange(num_heads)[:, None] == jnp.arange(width)[None, :] // head_width).astype(F32)

    def expand(value):
        return jnp.repeat(value, head_width, axis=-1)[None, :]

    def widen(value):
        return fdot(value, hot, NN, HIGHEST)

    def per_head(value):
        return fdot(value, hot, NT, HIGH)

    step_wide, local_wide, decay_wide = (widen(step_size), widen(log_local), widen(log_decay))
    log_row = log_row.reshape(width // PAIR, 2, bins)
    value_sig = jax.nn.sigmoid(value_raw)
    activated = value_raw * value_sig
    scaled_in = step_wide * activated
    total_wide = expand(log_total)
    tail_wide = jnp.exp(total_wide - decay_wide)
    tail_scaled = tail_wide * scaled_in
    state_local = fdot(in_map, tail_scaled, TN)
    state_in = carried_in(log_total, state_local, expand, False)

    result_local = core_forward(
        value_raw, step_wide, local_wide, log_row, in_map, in_t, out_map
    )
    grad_mixed = fdot(grad_output, output_full, NT, None)
    skip_wide = expand(head_params[2])
    decay_in = jnp.exp(decay_wide)
    result = result_local + decay_in * fdot(out_map, state_in, NN)
    ssd_out = result + skip_wide * activated
    gate_sig = jax.nn.sigmoid(gate_pre)
    gate_act = gate_pre * gate_sig
    gated = ssd_out * gate_act
    gate_scale = lax.rsqrt(jnp.mean(gated * gated, axis=-1, keepdims=True) + epsilon)
    gated_norm = gated * gate_scale
    mixed_out = (gated_norm * gate_full).astype(BF16)
    term_gate = jnp.sum(grad_mixed * gated_norm, axis=0) * grad_scale
    grad_gnorm = grad_mixed * gate_full
    grad_gated = gate_scale * (
        grad_gnorm - gated_norm * jnp.mean(grad_gnorm * gated_norm, axis=-1, keepdims=True)
    )
    grad_ssd = grad_gated * gate_act
    grad_gate = grad_gated * ssd_out * gate_sig * (1.0 + gate_pre * (1.0 - gate_sig))

    adjoint_local = fdot(out_map, decay_in * grad_ssd, TN)
    adjoint_out = carried_in(log_total, adjoint_local, expand, True)
    term_output = fdot(mixed_out, grad_output, TN, None) * grad_scale
    output_grad = scatter_sum(term_output, BF16)

    dx_local, din_local, dout = core_backward(
        value_raw,
        step_wide,
        local_wide,
        log_row,
        in_map,
        in_t,
        out_map,
        out_t,
        grad_ssd,
        state_in,
    )
    grad_scaled = dx_local + tail_wide * fdot(in_map, adjoint_out, NN)
    grad_in_map = din_local + fdot(tail_scaled, adjoint_out, NT)
    state_end = jnp.exp(total_wide) * state_in + state_local
    end_term = per_head(jnp.sum(state_end * adjoint_out, axis=0, keepdims=True))
    pull_step = per_head(activated * grad_scaled)
    pull_log = per_head(grad_ssd * result) - step_size * pull_step
    grad_rate = fdot(lower_all, pull_log, TN, HIGHEST) + end_term
    grad_step_size = pull_step - rate * grad_rate
    grad_step_raw = grad_step_size * jax.nn.sigmoid(step_in)
    grad_heads = jnp.stack(
        [
            jnp.sum(grad_step_raw, axis=0),
            jnp.sum(grad_rate * log_rate, axis=0),
            per_head(jnp.sum(grad_ssd * activated, axis=0, keepdims=True))[0],
        ]
    )
    grad_active = step_wide * grad_scaled + skip_wide * grad_ssd
    grad_value = grad_active * value_sig * (1.0 + value_raw * (1.0 - value_sig))
    grad_proj = jnp.concatenate(
        [
            grad_gate.astype(BF16),
            grad_value.astype(BF16),
            grad_in_map.astype(BF16),
            dout.astype(BF16),
        ],
        axis=1,
    )
    grad_step_low = grad_step_raw.astype(BF16)
    term_input = fdot(norm_act, grad_proj, TN, None) * grad_scale
    input_grad = scatter_sum(term_input, BF16)
    grad_act = fdot(grad_proj, input_full, NT, None) + fdot(grad_step_low, step_full, NT, None)
    term_step = fdot(norm_act, grad_step_low, TN, None) * grad_scale
    term_norm = jnp.sum(grad_act * normed, axis=0) * grad_scale
    grad_normed = grad_act * norm_full
    grad_input = in_scale * (
        grad_normed - normed * jnp.mean(grad_normed * normed, axis=-1, keepdims=True)
    )
    term_table = jnp.sum(grad_input, axis=0) * grad_scale

    small = jnp.concatenate(
        [term_norm[:, None], term_gate[:, None], term_step, term_table[:, None]], axis=1
    )
    core = lax.axis_index("ctx") % 2
    small = halve_core(blocks(small), core, F32)
    small = halve_chips(jnp.swapaxes(small, 0, 1), F32)
    session_hot = (session_ids[0] == jnp.arange(sessions)).astype(F32)
    table_part = small[:, :, -1:] * session_hot[None, None, :]
    small = halve_dp(jnp.concatenate([small[:, :, :-1], table_part], axis=2), F32)

    heads = grad_heads * grad_scale
    for bit in bits_of(context_count):
        heads = heads + swap_ctx(heads, bit)
    for stage in range(len(bits_of(data_count))):
        heads = heads + swap_dp(heads, stage)
    return (
        grad_input.astype(BF16)[None],
        small[:, 0],
        input_grad,
        small[:, 2 : 2 + num_heads],
        heads,
        small[:, 1],
        output_grad,
        small[:, 2 + num_heads :].T,
    )


def solution(mesh):
    placed = (
        P("dp", "ctx", None),
        P("dp", "ctx", None),
        P("dp"),
        P(),
        P("dp"),
        P("dp", None),
        P("dp", None),
        P(),
        P("dp"),
        P("dp", None),
    )
    return jax.shard_map(
        per_device,
        mesh=mesh,
        in_specs=placed,
        out_specs=(
            P("dp", "ctx", None),
            P(("dp", "ctx")),
            P(("dp", "ctx"), None),
            P(("dp", "ctx"), None),
            P(),
            P(("dp", "ctx")),
            P(("dp", "ctx"), None),
            P(None, ("dp", "ctx")),
        ),
        check_vma=False,
    )
```

```python
import functools
import math

import jax
import jax.numpy as jnp
from jax import lax
from jax.experimental import pallas as pl
from jax.experimental.pallas import tpu as pltpu
from jax.sharding import PartitionSpec as P

epsilon = 1e-05
CHUNK = 128
PAIR = 128
F32 = jnp.float32
BF16 = jnp.bfloat16
HIGHEST = lax.Precision.HIGHEST
HIGH = lax.Precision.HIGH
NN = (((1,), (0,)), ((), ()))
NT = (((1,), (1,)), ((), ()))
TN = (((0,), (0,)), ((), ()))


def split(value):
    high = value.astype(BF16)
    return (high, (value - high.astype(F32)).astype(BF16))


def dot3(left, right, dims):
    one = functools.partial(lax.dot_general, dimension_numbers=dims, preferred_element_type=F32)
    return one(left[0], right[0]) + (one(left[0], right[1]) + one(left[1], right[0]))


def chunk_rows(c):
    return slice(c * CHUNK, (c + 1) * CHUNK)


def forward_kernel(v_ref, dt_ref, log_ref, row_ref, in_ref, in_t_ref, out_ref, y_ref, scores):
    chunks = v_ref.shape[0] // CHUNK

    @pl.when(pl.program_id(0) == 0)
    def _():
        for c in range(chunks):
            rows = chunk_rows(c)
            scores[c] = dot3(split(out_ref[rows, :]), split(in_ref[rows, :]), NT)

    lane = lax.broadcasted_iota(jnp.int32, (CHUNK, PAIR), 1)
    later = lax.broadcasted_iota(jnp.int32, (CHUNK, CHUNK), 0)
    causal = later >= lax.broadcasted_iota(jnp.int32, (CHUNK, CHUNK), 1)
    state = None
    for c in range(chunks):
        rows = chunk_rows(c)
        v = v_ref[rows, :]
        scaled = dt_ref[rows, :] * (v * jax.nn.sigmoid(v))
        log = log_ref[rows, :]
        result = None
        for h in range(2):
            column = jnp.broadcast_to(log[:, h * 64 : h * 64 + 1], (CHUNK, CHUNK))
            gap = column - row_ref[0, h : h + 1, rows]
            weights = jnp.where(causal, jnp.exp(jnp.where(causal, gap, 0.0)), 0.0) * scores[c]
            mine = jnp.where((lane < 64) == (h == 0), scaled, 0.0)
            part = dot3(split(weights), split(mine), NN)
            result = part if result is None else result + part
        if state is not None:
            result = result + jnp.exp(log) * dot3(split(out_ref[rows, :]), split(state), NN)
        y_ref[rows, :] = result
        if c + 1 < chunks:
            last = log[CHUNK - 1 : CHUNK, :]
            fresh = dot3(split(in_t_ref[:, rows]), split(jnp.exp(last - log) * scaled), NN)
            state = fresh if state is None else jnp.exp(last) * state + fresh


def backward_kernel(
    v_ref,
    dt_ref,
    log_ref,
    row_ref,
    in_ref,
    in_t_ref,
    out_ref,
    out_t_ref,
    grad_ref,
    state_ref,
    dx_ref,
    din_ref,
    dout_ref,
    scores,
    dscores,
):
    chunks = v_ref.shape[0] // CHUNK
    step = pl.program_id(0)

    @pl.when(step == 0)
    def _():
        dscores[...] = jnp.zeros_like(dscores)
        din_ref[...] = jnp.zeros_like(din_ref)
        dout_ref[...] = jnp.zeros_like(dout_ref)
        for c in range(chunks):
            rows = chunk_rows(c)
            scores[c] = dot3(split(in_ref[rows, :]), split(out_ref[rows, :]), NT)

    lane = lax.broadcasted_iota(jnp.int32, (CHUNK, PAIR), 1)
    earlier = lax.broadcasted_iota(jnp.int32, (CHUNK, CHUNK), 0)
    causal = earlier <= lax.broadcasted_iota(jnp.int32, (CHUNK, CHUNK), 1)
    states = [state_ref[...]]
    inputs = []
    for c in range(chunks):
        rows = chunk_rows(c)
        v = v_ref[rows, :]
        scaled = dt_ref[rows, :] * (v * jax.nn.sigmoid(v))
        log = log_ref[rows, :]
        last = log[CHUNK - 1 : CHUNK, :]
        tail = jnp.exp(last - log)
        tailed = split(tail * scaled)
        inputs.append((scaled, log, last, tail, tailed))
        if c + 1 < chunks:
            fresh = dot3(split(in_t_ref[:, rows]), tailed, NN)
            states.append(jnp.exp(last) * states[c] + fresh)
    adjoint = None
    for c in reversed(range(chunks)):
        rows = chunk_rows(c)
        scaled, log, last, tail, tailed = inputs[c]
        grad = grad_ref[rows, :]
        grad_split = split(grad)
        decayed = split(jnp.exp(log) * grad)
        dout_ref[rows, :] += dot3(decayed, split(states[c]), NT)
        dx = None
        if adjoint is not None:
            adjoint_split = split(adjoint)
            dx = tail * dot3(split(in_ref[rows, :]), adjoint_split, NN)
            din_ref[rows, :] += dot3(tailed, adjoint_split, NT)
        total = dscores[c]
        for h in range(2):
            own = (lane < 64) == (h == 0)
            column = jnp.broadcast_to(log[:, h * 64 : h * 64 + 1], (CHUNK, CHUNK))
            gap = row_ref[0, h : h + 1, rows] - column
            decay = jnp.where(causal, jnp.exp(jnp.where(causal, gap, 0.0)), 0.0)
            mine = split(jnp.where(own, grad, 0.0))
            part = dot3(split(decay * scores[c]), mine, NN)
            dx = part if dx is None else dx + part
            total = total + decay * dot3(split(scaled), mine, NT)
        dscores[c] = total
        dx_ref[rows, :] = dx
        if c > 0:
            fresh = dot3(split(out_t_ref[:, rows]), decayed, NN)
            adjoint = fresh if adjoint is None else jnp.exp(last) * adjoint + fresh

    @pl.when(step == pl.num_programs(0) - 1)
    def _():
        for c in range(chunks):
            rows = chunk_rows(c)
            total = split(dscores[c])
            din_ref[rows, :] += dot3(total, split(out_ref[rows, :]), NN)
            dout_ref[rows, :] += dot3(total, split(in_ref[rows, :]), TN)


def pair_block(bins):
    return pl.BlockSpec((bins, PAIR), lambda j: (0, j))


def whole(shape):
    return pl.BlockSpec(shape, lambda j: (0,) * len(shape))


def core_forward(v, dt, log, row, in_map, in_t, out_map):
    bins, width = v.shape
    pairs, chunks = width // PAIR, bins // CHUNK
    block = pair_block(bins)
    return pl.pallas_call(
        forward_kernel,
        grid=(pairs,),
        out_shape=jax.ShapeDtypeStruct((bins, width), F32),
        in_specs=[
            block,
            block,
            block,
            pl.BlockSpec((1, 2, bins), lambda j: (j, 0, 0)),
            whole(in_map.shape),
            whole(in_t.shape),
            whole(out_map.shape),
        ],
        out_specs=block,
        scratch_shapes=[pltpu.VMEM((chunks, CHUNK, CHUNK), F32)],
        compiler_params=pltpu.CompilerParams(vmem_limit_bytes=40 * 1024 * 1024),
        cost_estimate=pl.CostEstimate(
            flops=pairs * chunks * 36 * 128**3, bytes_accessed=16 * bins * width, transcendentals=0
        ),
        name="core_forward",
    )(v, dt, log, row, in_map, in_t, out_map)


def core_backward(v, dt, log, row, in_map, in_t, out_map, out_t, grad, state):
    bins, width = v.shape
    pairs, chunks = width // PAIR, bins // CHUNK
    block = pair_block(bins)
    return pl.pallas_call(
        backward_kernel,
        grid=(pairs,),
        out_shape=[
            jax.ShapeDtypeStruct((bins, width), F32),
            jax.ShapeDtypeStruct(in_map.shape, F32),
            jax.ShapeDtypeStruct(out_map.shape, F32),
        ],
        in_specs=[
            block,
            block,
            block,
            pl.BlockSpec((1, 2, bins), lambda j: (j, 0, 0)),
            whole(in_map.shape),
            whole(in_t.shape),
            whole(out_map.shape),
            whole(out_t.shape),
            block,
            pl.BlockSpec((state.shape[0], PAIR), lambda j: (0, j)),
        ],
        out_specs=[block, whole(in_map.shape), whole(out_map.shape)],
        scratch_shapes=[
            pltpu.VMEM((chunks, CHUNK, CHUNK), F32),
            pltpu.VMEM((chunks, CHUNK, CHUNK), F32),
        ],
        compiler_params=pltpu.CompilerParams(vmem_limit_bytes=40 * 1024 * 1024),
        cost_estimate=pl.CostEstimate(
            flops=pairs * chunks * 80 * 128**3, bytes_accessed=24 * bins * width, transcendentals=0
        ),
        name="core_backward",
    )(v, dt, log, row, in_map, in_t, out_map, out_t, grad, state)


def swap_ctx(value, bit):
    count = lax.axis_size("ctx")
    return lax.ppermute(value, "ctx", [(i, i ^ bit) for i in range(count)])


def bits_of(count):
    return [1 << b for b in range(count.bit_length() - 1)]


def dp_order(core):
    bits = bits_of(lax.axis_size("dp"))
    return bits if core == 0 else bits[::-1]


def swap_dp(value, stage):
    data_count, context_count = lax.axis_size("dp"), lax.axis_size("ctx")
    pairs = []
    for d in range(data_count):
        for c in range(context_count):
            partner = d ^ dp_order(c % 2)[stage]
            pairs.append((d * context_count + c, partner * context_count + c))
    return lax.ppermute(value, ("dp", "ctx"), pairs)


def dp_masks(core):
    first, second = dp_order(0), dp_order(1)
    return [jnp.where(core == 0, a, b) for a, b in zip(first, second)]


def pick(value, index, axis=0):
    return lax.dynamic_index_in_dim(value, index, axis, keepdims=False)


def reorder(term, mine, masks):
    relative = [0]
    for mask in masks[::-1]:
        relative = relative + [r ^ mask for r in relative]
    return jnp.stack([pick(term, mine ^ r) for r in relative])


def halve(terms, mine, masks, swap):
    terms = [reorder(term, mine, masks) for term in terms]
    for stage in range(len(masks)):
        half = terms[0].shape[0] // 2
        message = [terms[0][half:].astype(BF16)]
        for term in terms[1:]:
            high = lax.reduce_precision(term[half:], 8, 7)
            message = message + [high.astype(BF16), (term[half:] - high).astype(BF16)]
        message = yield jnp.concatenate(message, axis=-1)
        got = yield swap(message, stage)
        got = got.astype(F32)
        wide = terms[0].shape[-1]
        kept = [terms[0][:half] + got[..., :wide]]
        for term in terms[1:]:
            size = term.shape[-1]
            rider = got[..., wide : wide + size] + got[..., wide + size : wide + 2 * size]
            kept.append(term[:half] + rider)
            wide += 2 * size
        terms = kept
    return [term[0] for term in terms]


def halve_core(term, wire):
    core = lax.axis_index("ctx") % 2
    got = swap_ctx(pick(term, 1 - core, 2).astype(wire), 1)
    return pick(term, core, 2) + got.astype(F32)


def halve_dp(terms):
    core = lax.axis_index("ctx") % 2
    return (yield from halve(terms, lax.axis_index("dp"), dp_masks(core), swap_dp))


def halve_chips(terms):
    bits = bits_of(lax.axis_size("ctx") // 2)
    swap = lambda value, stage: swap_ctx(value, 2 * bits[stage])
    return (yield from halve(terms, lax.axis_index("ctx") // 2, bits, swap))


def blocks(term):
    data_count, context_count = lax.axis_size("dp"), lax.axis_size("ctx")
    rows = term.shape[0] // (data_count * context_count)
    return term.reshape((data_count, context_count // 2, 2, rows) + term.shape[1:])


def scatter_steps(term, rider=None):
    terms = [halve_core(blocks(term), BF16)]
    if rider is not None:
        terms.append(halve_core(blocks(rider), F32))
    terms = yield from halve_dp(terms)
    return (yield from halve_chips(terms))


def finish(steps, value):
    try:
        while True:
            value = steps.send(value)
    except StopIteration as ending:
        return ending.value


def gather_rows(shard):
    data_count = lax.axis_size("dp")
    mine, core = lax.axis_index("dp"), lax.axis_index("ctx") % 2
    half = shard.shape[0] // 2
    held = lax.dynamic_slice_in_dim(shard, core * half, half, 0)[None]
    where = [mine]
    for stage, mask in enumerate(dp_masks(core)):
        held = jnp.concatenate([held, swap_dp(held, stage)])
        where = where + [w ^ mask for w in where]
    other = swap_ctx(held, 1)
    their_where = [mine]
    for mask in dp_masks(1 - core):
        their_where = their_where + [w ^ mask for w in their_where]
    full = jnp.zeros((data_count, 2) + held.shape[1:], shard.dtype)
    for i in range(data_count):
        full = lax.dynamic_update_slice(full, held[i][None, None], (where[i], core, 0, 0))
        full = lax.dynamic_update_slice(
            full, other[i][None, None], (their_where[i], 1 - core, 0, 0)
        )
    return full.reshape((-1,) + shard.shape[1:])


def carried_in(log_total, state, expand, backward, beside=None):
    mine = lax.axis_index("ctx")
    core = mine % 2
    half = state.shape[0] // 2

    def is_after(bit):
        is_high = (mine & bit) != 0
        return jnp.logical_not(is_high) if backward else is_high

    partner = swap_ctx(state, 1)
    partner_log = swap_ctx(log_total, 1)
    late = is_after(1)
    late_log = jnp.where(late, log_total, partner_log)
    own_half = lax.dynamic_slice_in_dim(state, core * half, half, 0)
    partner_half = lax.dynamic_slice_in_dim(partner, core * half, half, 0)
    early_half = jnp.where(late, partner_half, own_half)
    late_half = jnp.where(late, own_half, partner_half)
    total = jnp.exp(expand(late_log)) * early_half + late_half
    total_log = log_total + partner_log
    prefix_log, prefix = jnp.zeros_like(log_total), jnp.zeros_like(total)
    extra = None
    for bit in bits_of(lax.axis_size("ctx"))[1:]:
        got = swap_ctx(total, bit)
        if beside is not None and 2 * bit == lax.axis_size("ctx"):
            extra, got = lax.optimization_barrier((beside(total), got))
        got_log = swap_ctx(total_log, bit)
        after = is_after(bit)
        prefix = jnp.where(after, jnp.exp(expand(prefix_log)) * got + prefix, prefix)
        prefix_log = jnp.where(after, prefix_log + got_log, prefix_log)
        joined_mine = jnp.exp(expand(total_log)) * got + total
        total = jnp.where(after, joined_mine, jnp.exp(expand(got_log)) * total + got)
        total_log = total_log + got_log
    other = swap_ctx(prefix, 1)
    first = jnp.where(core == 0, prefix, other)
    second = jnp.where(core == 0, other, prefix)
    whole_prefix = jnp.concatenate([first, second], axis=0)
    joined = jnp.where(late, jnp.exp(expand(partner_log)) * whole_prefix + partner, whole_prefix)
    return (joined, extra)


def fdot(left, right, dims, precision=HIGH):
    return lax.dot_general(left, right, dims, precision=precision, preferred_element_type=F32)


def per_device(
    tokens,
    grad_output,
    session_ids,
    session_table,
    norm_gain,
    input_weight,
    step_weight,
    head_params,
    gate_gain,
    output_weight,
):
    data_count, context_count = lax.axis_size("dp"), lax.axis_size("ctx")
    num_seqs, bins, model_width = tokens.shape
    assert num_seqs == 1
    width = output_weight.shape[0] * data_count
    num_heads = step_weight.shape[1]
    head_width = width // num_heads
    state_width = (input_weight.shape[1] - 2 * width) // 2
    sessions = session_table.shape[0]
    chunks = bins // CHUNK
    grad_scale = 1.0 / math.sqrt(bins * data_count * context_count)
    tokens, grad_output = tokens[0], grad_output[0]

    session_low = jnp.broadcast_to(session_ids.astype(BF16)[None, :], (step_weight.shape[0], 1))
    side = jnp.concatenate(
        [step_weight, norm_gain[:, None], gate_gain[:, None], session_low], axis=1
    )
    side_full = gather_rows(side)
    input_full = gather_rows(input_weight)
    output_full = gather_rows(output_weight)
    step_full = side_full[:, :num_heads]
    norm_full = side_full[:, num_heads].astype(F32)[None, :]
    gate_full = side_full[:, num_heads + 1].astype(F32)[None, :]
    all_sessions = side_full[:: step_weight.shape[0], num_heads + 2].astype(jnp.int32)

    table_row = lax.dynamic_slice_in_dim(session_table, session_ids[0], 1, 0).astype(F32)
    layer_in = tokens.astype(F32) + table_row
    in_scale = lax.rsqrt(jnp.mean(layer_in * layer_in, axis=-1, keepdims=True) + epsilon)
    normed = layer_in * in_scale
    norm_act = (normed * norm_full).astype(BF16)
    projected = fdot(norm_act, input_full, NN, None)
    step_raw = fdot(norm_act, step_full, NN, None)
    gate_pre = projected[:, :width]
    value_raw = projected[:, width : 2 * width]
    in_map = projected[:, 2 * width : 2 * width + state_width]
    out_map = projected[:, 2 * width + state_width :]
    in_t, out_t = in_map.T, out_map.T

    step_in = step_raw + head_params[0][None, :]
    step_size = jax.nn.softplus(step_in)
    rate = jnp.exp(head_params[1])[None, :]
    log_rate = -rate * step_size
    position = jnp.arange(bins)
    lower = position[:, None] >= position[None, :]
    same = (position[:, None] // CHUNK) == (position[None, :] // CHUNK)
    lower_all = lower.astype(F32)
    lower_chunk = (lower & same).astype(F32)
    log_local = fdot(lower_chunk, log_rate, NN, HIGHEST)
    log_row = fdot(log_rate, lower_chunk, (((0,), (1,)), ((), ())), HIGHEST)
    log_decay = fdot(lower_all, log_rate, NN, HIGHEST)
    log_total = jnp.sum(log_rate, axis=0)
    hot = (jnp.arange(num_heads)[:, None] == jnp.arange(width)[None, :] // head_width).astype(F32)

    def expand(value):
        return jnp.repeat(value, head_width, axis=-1)[None, :]

    def widen(value):
        return fdot(value, hot, NN, HIGHEST)

    def per_head(value):
        return fdot(value, hot, NT, HIGH)

    step_wide, local_wide, decay_wide = (widen(step_size), widen(log_local), widen(log_decay))
    log_row = log_row.reshape(width // PAIR, 2, bins)
    value_sig = jax.nn.sigmoid(value_raw)
    activated = value_raw * value_sig
    scaled_in = step_wide * activated
    total_wide = expand(log_total)
    tail_wide = jnp.exp(total_wide - decay_wide)
    tail_scaled = tail_wide * scaled_in
    state_local = fdot(in_map, tail_scaled, TN)

    def beside(ready):
        local, ready = lax.optimization_barrier((local_wide, ready))
        return core_forward(value_raw, step_wide, local, log_row, in_map, in_t, out_map)

    state_in, result_local = carried_in(log_total, state_local, expand, False, beside)
    grad_mixed = fdot(grad_output, output_full, NT, None)
    skip_wide = expand(head_params[2])
    decay_in = jnp.exp(decay_wide)
    result = result_local + decay_in * fdot(out_map, state_in, NN)
    ssd_out = result + skip_wide * activated
    gate_sig = jax.nn.sigmoid(gate_pre)
    gate_act = gate_pre * gate_sig
    gated = ssd_out * gate_act
    gate_scale = lax.rsqrt(jnp.mean(gated * gated, axis=-1, keepdims=True) + epsilon)
    gated_norm = gated * gate_scale
    mixed_out = (gated_norm * gate_full).astype(BF16)
    term_gate = jnp.sum(grad_mixed * gated_norm, axis=0) * grad_scale
    grad_gnorm = grad_mixed * gate_full
    grad_gated = gate_scale * (
        grad_gnorm - gated_norm * jnp.mean(grad_gnorm * gated_norm, axis=-1, keepdims=True)
    )
    grad_ssd = grad_gated * gate_act
    grad_gate = grad_gated * ssd_out * gate_sig * (1.0 + gate_pre * (1.0 - gate_sig))

    adjoint_local = fdot(out_map, decay_in * grad_ssd, TN)
    grad_gate_low = grad_gate.astype(BF16)
    term_output = fdot(mixed_out, grad_output, TN, None) * grad_scale
    term_gate_in = fdot(norm_act, grad_gate_low, TN, None) * grad_scale
    early = scatter_steps(jnp.concatenate([term_output, term_gate_in], axis=1))
    first = next(early)

    def beside_adjoint(ready):
        local, ready, message = lax.optimization_barrier((local_wide, ready, first))
        outputs = core_backward(
            value_raw,
            step_wide,
            local,
            log_row,
            in_map,
            in_t,
            out_map,
            out_t,
            grad_ssd,
            state_in,
        )
        return lax.optimization_barrier((outputs, early.send(message)))

    adjoint_out, (outputs, got) = carried_in(
        log_total, adjoint_local, expand, True, beside_adjoint
    )
    dx_local, din_local, dout = outputs
    message = early.send(got)
    dx_local, message = lax.optimization_barrier((dx_local, message))
    got = early.send(message)
    grad_scaled = dx_local + tail_wide * fdot(in_map, adjoint_out, NN)
    grad_in_map = din_local + fdot(tail_scaled, adjoint_out, NT)
    state_end = jnp.exp(total_wide) * state_in + state_local
    end_term = per_head(jnp.sum(state_end * adjoint_out, axis=0, keepdims=True))
    pull_step = per_head(activated * grad_scaled)
    pull_log = per_head(grad_ssd * result) - step_size * pull_step
    grad_rate = fdot(lower_all, pull_log, TN, HIGHEST) + end_term
    grad_step_size = pull_step - rate * grad_rate
    grad_step_raw = grad_step_size * jax.nn.sigmoid(step_in)
    grad_heads = jnp.stack(
        [
            jnp.sum(grad_step_raw, axis=0),
            jnp.sum(grad_rate * log_rate, axis=0),
            per_head(jnp.sum(grad_ssd * activated, axis=0, keepdims=True))[0],
        ]
    )
    grad_active = step_wide * grad_scaled + skip_wide * grad_ssd
    grad_value = grad_active * value_sig * (1.0 + value_raw * (1.0 - value_sig))
    grad_late = jnp.concatenate(
        [grad_value.astype(BF16), grad_in_map.astype(BF16), dout.astype(BF16)], axis=1
    )
    grad_step_low = grad_step_raw.astype(BF16)
    grad_late, got = lax.optimization_barrier((grad_late, got))
    message = early.send(got)
    grad_late, message = lax.optimization_barrier((grad_late, message))
    got = early.send(message)
    term_late = fdot(norm_act, grad_late, TN, None) * grad_scale
    grad_act = (
        fdot(grad_gate_low, input_full[:, :width], NT, None)
        + fdot(grad_late, input_full[:, width:], NT, None)
        + fdot(grad_step_low, step_full, NT, None)
    )
    term_step = fdot(norm_act, grad_step_low, TN, None) * grad_scale
    term_norm = jnp.sum(grad_act * normed, axis=0) * grad_scale
    grad_normed = grad_act * norm_full
    grad_input = in_scale * (
        grad_normed - normed * jnp.mean(grad_normed * normed, axis=-1, keepdims=True)
    )
    term_table = jnp.sum(grad_input, axis=0) * grad_scale

    rows = model_width // (data_count * context_count)
    head_columns = -(-grad_heads.size // rows)
    heads = jnp.zeros((head_columns * rows,), F32).at[: grad_heads.size].set(grad_heads.ravel())
    heads = jnp.tile(heads.reshape(head_columns, rows).T * grad_scale, (model_width // rows, 1))
    slot = (jnp.arange(data_count) == lax.axis_index("dp")).astype(F32)
    rider = jnp.concatenate(
        [
            term_norm[:, None],
            term_gate[:, None],
            term_step,
            heads,
            term_table[:, None] * slot[None, :],
        ],
        axis=1,
    )
    late_steps = scatter_steps(term_late, rider)
    late, rider = finish(late_steps, next(late_steps))
    early = finish(early, got)[0]
    output_grad = early[:, :model_width]
    split_at = 2 + num_heads
    heads = rider[:, split_at : split_at + head_columns].T.ravel()[: grad_heads.size]
    session_hot = (all_sessions[:, None] == jnp.arange(sessions)[None, :]).astype(F32)
    table_grad = fdot(session_hot, rider[:, split_at + head_columns :], (((0,), (1,)), ((), ())), HIGHEST)
    return (
        grad_input.astype(BF16)[None],
        rider[:, 0],
        jnp.concatenate([early[:, model_width:], late], axis=1),
        rider[:, 2:split_at],
        heads.reshape(grad_heads.shape),
        rider[:, 1],
        output_grad,
        table_grad,
    )


def solution(mesh):
    placed = (
        P("dp", "ctx", None),
        P("dp", "ctx", None),
        P("dp"),
        P(),
        P("dp"),
        P("dp", None),
        P("dp", None),
        P(),
        P("dp"),
        P("dp", None),
    )
    return jax.shard_map(
        per_device,
        mesh=mesh,
        in_specs=placed,
        out_specs=(
            P("dp", "ctx", None),
            P(("dp", "ctx")),
            P(("dp", "ctx"), None),
            P(("dp", "ctx"), None),
            P(),
            P(("dp", "ctx")),
            P(("dp", "ctx"), None),
            P(None, ("dp", "ctx")),
        ),
        check_vma=False,
    )
```

```python
import functools
import math

import jax
import jax.numpy as jnp
from jax import lax
from jax.experimental import pallas as pl
from jax.experimental.pallas import tpu as pltpu
from jax.sharding import PartitionSpec as P

epsilon = 1e-05
CHUNK = 128
PAIR = 128
F32 = jnp.float32
BF16 = jnp.bfloat16
HIGHEST = lax.Precision.HIGHEST
HIGH = lax.Precision.HIGH
NN = (((1,), (0,)), ((), ()))
NT = (((1,), (1,)), ((), ()))
TN = (((0,), (0,)), ((), ()))


def split(value):
    high = value.astype(BF16)
    return (high, (value - high.astype(F32)).astype(BF16))


def dot3(left, right, dims):
    one = functools.partial(lax.dot_general, dimension_numbers=dims, preferred_element_type=F32)
    return one(left[0], right[0]) + (one(left[0], right[1]) + one(left[1], right[0]))


def chunk_rows(c):
    return slice(c * CHUNK, (c + 1) * CHUNK)


def forward_kernel(v_ref, dt_ref, log_ref, row_ref, in_ref, in_t_ref, out_ref, y_ref, scores):
    chunks = v_ref.shape[0] // CHUNK

    @pl.when(pl.program_id(0) == 0)
    def _():
        for c in range(chunks):
            rows = chunk_rows(c)
            scores[c] = dot3(split(out_ref[rows, :]), split(in_ref[rows, :]), NT)

    lane = lax.broadcasted_iota(jnp.int32, (CHUNK, PAIR), 1)
    later = lax.broadcasted_iota(jnp.int32, (CHUNK, CHUNK), 0)
    causal = later >= lax.broadcasted_iota(jnp.int32, (CHUNK, CHUNK), 1)
    state = None
    for c in range(chunks):
        rows = chunk_rows(c)
        v = v_ref[rows, :]
        scaled = dt_ref[rows, :] * (v * jax.nn.sigmoid(v))
        log = log_ref[rows, :]
        result = None
        for h in range(2):
            column = jnp.broadcast_to(log[:, h * 64 : h * 64 + 1], (CHUNK, CHUNK))
            gap = column - row_ref[0, h : h + 1, rows]
            weights = jnp.where(causal, jnp.exp(jnp.where(causal, gap, 0.0)), 0.0) * scores[c]
            mine = jnp.where((lane < 64) == (h == 0), scaled, 0.0)
            part = dot3(split(weights), split(mine), NN)
            result = part if result is None else result + part
        if state is not None:
            result = result + jnp.exp(log) * dot3(split(out_ref[rows, :]), split(state), NN)
        y_ref[rows, :] = result
        if c + 1 < chunks:
            last = log[CHUNK - 1 : CHUNK, :]
            fresh = dot3(split(in_t_ref[:, rows]), split(jnp.exp(last - log) * scaled), NN)
            state = fresh if state is None else jnp.exp(last) * state + fresh


def backward_kernel(
    v_ref,
    dt_ref,
    log_ref,
    row_ref,
    in_ref,
    in_t_ref,
    out_ref,
    out_t_ref,
    grad_ref,
    state_ref,
    dx_ref,
    din_ref,
    dout_ref,
    scores,
    dscores,
):
    chunks = v_ref.shape[0] // CHUNK
    step = pl.program_id(0)

    @pl.when(step == 0)
    def _():
        dscores[...] = jnp.zeros_like(dscores)
        din_ref[...] = jnp.zeros_like(din_ref)
        dout_ref[...] = jnp.zeros_like(dout_ref)
        for c in range(chunks):
            rows = chunk_rows(c)
            scores[c] = dot3(split(in_ref[rows, :]), split(out_ref[rows, :]), NT)

    lane = lax.broadcasted_iota(jnp.int32, (CHUNK, PAIR), 1)
    earlier = lax.broadcasted_iota(jnp.int32, (CHUNK, CHUNK), 0)
    causal = earlier <= lax.broadcasted_iota(jnp.int32, (CHUNK, CHUNK), 1)
    states = [state_ref[...]]
    inputs = []
    for c in range(chunks):
        rows = chunk_rows(c)
        v = v_ref[rows, :]
        scaled = dt_ref[rows, :] * (v * jax.nn.sigmoid(v))
        log = log_ref[rows, :]
        last = log[CHUNK - 1 : CHUNK, :]
        tail = jnp.exp(last - log)
        tailed = split(tail * scaled)
        inputs.append((scaled, log, last, tail, tailed))
        if c + 1 < chunks:
            fresh = dot3(split(in_t_ref[:, rows]), tailed, NN)
            states.append(jnp.exp(last) * states[c] + fresh)
    adjoint = None
    for c in reversed(range(chunks)):
        rows = chunk_rows(c)
        scaled, log, last, tail, tailed = inputs[c]
        grad = grad_ref[rows, :]
        grad_split = split(grad)
        decayed = split(jnp.exp(log) * grad)
        dout_ref[rows, :] += dot3(decayed, split(states[c]), NT)
        dx = None
        if adjoint is not None:
            adjoint_split = split(adjoint)
            dx = tail * dot3(split(in_ref[rows, :]), adjoint_split, NN)
            din_ref[rows, :] += dot3(tailed, adjoint_split, NT)
        total = dscores[c]
        for h in range(2):
            own = (lane < 64) == (h == 0)
            column = jnp.broadcast_to(log[:, h * 64 : h * 64 + 1], (CHUNK, CHUNK))
            gap = row_ref[0, h : h + 1, rows] - column
            decay = jnp.where(causal, jnp.exp(jnp.where(causal, gap, 0.0)), 0.0)
            mine = split(jnp.where(own, grad, 0.0))
            part = dot3(split(decay * scores[c]), mine, NN)
            dx = part if dx is None else dx + part
            total = total + decay * dot3(split(scaled), mine, NT)
        dscores[c] = total
        dx_ref[rows, :] = dx
        if c > 0:
            fresh = dot3(split(out_t_ref[:, rows]), decayed, NN)
            adjoint = fresh if adjoint is None else jnp.exp(last) * adjoint + fresh

    @pl.when(step == pl.num_programs(0) - 1)
    def _():
        for c in range(chunks):
            rows = chunk_rows(c)
            total = split(dscores[c])
            din_ref[rows, :] += dot3(total, split(out_ref[rows, :]), NN)
            dout_ref[rows, :] += dot3(total, split(in_ref[rows, :]), TN)


def pair_block(bins):
    return pl.BlockSpec((bins, PAIR), lambda j: (0, j))


def whole(shape):
    return pl.BlockSpec(shape, lambda j: (0,) * len(shape))


def core_forward(v, dt, log, row, in_map, in_t, out_map):
    bins, width = v.shape
    pairs, chunks = width // PAIR, bins // CHUNK
    block = pair_block(bins)
    return pl.pallas_call(
        forward_kernel,
        grid=(pairs,),
        out_shape=jax.ShapeDtypeStruct((bins, width), F32),
        in_specs=[
            block,
            block,
            block,
            pl.BlockSpec((1, 2, bins), lambda j: (j, 0, 0)),
            whole(in_map.shape),
            whole(in_t.shape),
            whole(out_map.shape),
        ],
        out_specs=block,
        scratch_shapes=[pltpu.VMEM((chunks, CHUNK, CHUNK), F32)],
        compiler_params=pltpu.CompilerParams(vmem_limit_bytes=40 * 1024 * 1024),
        cost_estimate=pl.CostEstimate(
            flops=pairs * chunks * 36 * 128**3, bytes_accessed=16 * bins * width, transcendentals=0
        ),
        name="core_forward",
    )(v, dt, log, row, in_map, in_t, out_map)


def core_backward(v, dt, log, row, in_map, in_t, out_map, out_t, grad, state):
    bins, width = v.shape
    pairs, chunks = width // PAIR, bins // CHUNK
    block = pair_block(bins)
    return pl.pallas_call(
        backward_kernel,
        grid=(pairs,),
        out_shape=[
            jax.ShapeDtypeStruct((bins, width), F32),
            jax.ShapeDtypeStruct(in_map.shape, F32),
            jax.ShapeDtypeStruct(out_map.shape, F32),
        ],
        in_specs=[
            block,
            block,
            block,
            pl.BlockSpec((1, 2, bins), lambda j: (j, 0, 0)),
            whole(in_map.shape),
            whole(in_t.shape),
            whole(out_map.shape),
            whole(out_t.shape),
            block,
            pl.BlockSpec((state.shape[0], PAIR), lambda j: (0, j)),
        ],
        out_specs=[block, whole(in_map.shape), whole(out_map.shape)],
        scratch_shapes=[
            pltpu.VMEM((chunks, CHUNK, CHUNK), F32),
            pltpu.VMEM((chunks, CHUNK, CHUNK), F32),
        ],
        compiler_params=pltpu.CompilerParams(vmem_limit_bytes=40 * 1024 * 1024),
        cost_estimate=pl.CostEstimate(
            flops=pairs * chunks * 80 * 128**3, bytes_accessed=24 * bins * width, transcendentals=0
        ),
        name="core_backward",
    )(v, dt, log, row, in_map, in_t, out_map, out_t, grad, state)


def swap_ctx(value, bit):
    count = lax.axis_size("ctx")
    return lax.ppermute(value, "ctx", [(i, i ^ bit) for i in range(count)])


def bits_of(count):
    return [1 << b for b in range(count.bit_length() - 1)]


def dp_order(core):
    bits = bits_of(lax.axis_size("dp"))
    return bits if core == 0 else bits[::-1]


def swap_dp(value, stage):
    data_count, context_count = lax.axis_size("dp"), lax.axis_size("ctx")
    pairs = []
    for d in range(data_count):
        for c in range(context_count):
            partner = d ^ dp_order(c % 2)[stage]
            pairs.append((d * context_count + c, partner * context_count + c))
    return lax.ppermute(value, ("dp", "ctx"), pairs)


def dp_masks(core):
    first, second = dp_order(0), dp_order(1)
    return [jnp.where(core == 0, a, b) for a, b in zip(first, second)]


def pick(value, index, axis=0):
    return lax.dynamic_index_in_dim(value, index, axis, keepdims=False)


def reorder(term, mine, masks):
    relative = [0]
    for mask in masks[::-1]:
        relative = relative + [r ^ mask for r in relative]
    return jnp.stack([pick(term, mine ^ r) for r in relative])


def halve(terms, mine, masks, swap):
    terms = [(reorder(term, mine, masks), exact) for term, exact in terms]
    for stage in range(len(masks)):
        half = terms[0][0].shape[0] // 2
        message = []
        for term, exact in terms:
            if exact:
                high = lax.reduce_precision(term[half:], 8, 7)
                message += [high.astype(BF16), (term[half:] - high).astype(BF16)]
            else:
                message.append(term[half:].astype(BF16))
        message = yield jnp.concatenate(message, axis=-1)
        got = yield swap(message, stage)
        got = got.astype(F32)
        kept, at = [], 0
        for term, exact in terms:
            size = term.shape[-1]
            part = got[..., at : at + size]
            at += size
            if exact:
                part = part + got[..., at : at + size]
                at += size
            kept.append((term[:half] + part, exact))
        terms = kept
    return [(term[0], exact) for term, exact in terms]


def halve_core(term, wire):
    core = lax.axis_index("ctx") % 2
    got = swap_ctx(pick(term, 1 - core, 2).astype(wire), 1)
    return pick(term, core, 2) + got.astype(F32)


def halve_dp(terms):
    core = lax.axis_index("ctx") % 2
    return (yield from halve(terms, lax.axis_index("dp"), dp_masks(core), swap_dp))


def halve_chips(terms):
    bits = bits_of(lax.axis_size("ctx") // 2)
    swap = lambda value, stage: swap_ctx(value, 2 * bits[stage])
    return (yield from halve(terms, lax.axis_index("ctx") // 2, bits, swap))


def blocks(term):
    data_count, context_count = lax.axis_size("dp"), lax.axis_size("ctx")
    rows = term.shape[0] // (data_count * context_count)
    return term.reshape((data_count, context_count // 2, 2, rows) + term.shape[1:])


def scatter_steps(wide, riders=()):
    terms = [(halve_core(blocks(term), BF16), False) for term in wide]
    terms += [(halve_core(blocks(term), F32), True) for term in riders]
    terms = yield from halve_dp(terms)
    terms = yield from halve_chips(terms)
    return [term for term, exact in terms]


def finish(steps, value):
    try:
        while True:
            value = steps.send(value)
    except StopIteration as ending:
        return ending.value


def gather_kernel(data_count, *refs):
    arrays = (len(refs) - 5) // 2
    shards, fulls = refs[:arrays], refs[arrays : 2 * arrays]
    send_sem, recv_sem, pass_send, pass_recv, own_sem = refs[2 * arrays :]
    mine, place = lax.axis_index("dp"), lax.axis_index("ctx")
    core = lax.rem(place, 2)
    bits = [1 << b for b in range(data_count.bit_length() - 1)]

    def flip_bit(value, bit):
        return value + bit * (1 - 2 * lax.rem(lax.div(value, bit), 2))

    def flip(value, stage):
        first = flip_bit(value, bits[stage])
        second = flip_bit(value, bits[len(bits) - 1 - stage])
        return first * (1 - core) + second * core

    def origin(k):
        value = mine
        for stage in range(len(bits)):
            if k & (1 << stage):
                value = flip(value, stage)
        return value

    def rows_of(a, k):
        rows = shards[a].shape[0]
        start = origin(k) * rows + core * (rows // 2)
        return pl.ds(pl.multiple_of(start, rows // 2), rows // 2)

    def held(a, k):
        if k > 0:
            return fulls[a].at[rows_of(a, k)]
        half = shards[a].shape[0] // 2
        return shards[a].at[pl.ds(pl.multiple_of(core * half, half), half)]

    other = place + 1 - 2 * core

    def outgoing(a, k):
        stage = k.bit_length() - 1
        before = k - (1 << stage)
        return pltpu.make_async_remote_copy(
            src_ref=held(a, before),
            dst_ref=fulls[a].at[rows_of(a, before)],
            send_sem=send_sem.at[a, k],
            recv_sem=recv_sem.at[a, k],
            device_id=(flip(mine, stage), place),
            device_id_type=pl.DeviceIdType.MESH,
        )

    def incoming(a, k):
        return pltpu.make_async_remote_copy(
            src_ref=held(a, 0),
            dst_ref=fulls[a].at[rows_of(a, k)],
            send_sem=send_sem.at[a, k],
            recv_sem=recv_sem.at[a, k],
            device_id=(flip(mine, k.bit_length() - 1), place),
            device_id_type=pl.DeviceIdType.MESH,
        )

    def passed(a, k):
        return pltpu.make_async_remote_copy(
            src_ref=fulls[a].at[rows_of(a, k)],
            dst_ref=fulls[a].at[rows_of(a, k)],
            send_sem=pass_send.at[a, k],
            recv_sem=pass_recv.at[a, k],
            device_id=(mine, other),
            device_id_type=pl.DeviceIdType.MESH,
        )

    def pass_in(a, k):
        rows = shards[a].shape[0]
        value = mine
        for stage in range(len(bits)):
            if k & (1 << stage):
                first = flip_bit(value, bits[stage])
                second = flip_bit(value, bits[len(bits) - 1 - stage])
                value = first * core + second * (1 - core)
        start = value * rows + (1 - core) * (rows // 2)
        return pltpu.make_async_remote_copy(
            src_ref=held(a, 0),
            dst_ref=fulls[a].at[pl.ds(pl.multiple_of(start, rows // 2), rows // 2)],
            send_sem=pass_send.at[a, k],
            recv_sem=pass_recv.at[a, k],
            device_id=(mine, other),
            device_id_type=pl.DeviceIdType.MESH,
        )

    def own(a):
        rows = shards[a].shape[0]
        start = pl.multiple_of(mine * rows, rows)
        return pltpu.make_async_copy(shards[a], fulls[a].at[pl.ds(start, rows)], own_sem.at[a])

    barrier = pltpu.get_barrier_semaphore()
    partners = [(flip(mine, stage), place) for stage in range(len(bits))] + [(mine, other)]
    for partner in partners:
        pl.semaphore_signal(
            barrier, inc=1, device_id=partner, device_id_type=pl.DeviceIdType.MESH
        )
    pl.semaphore_wait(barrier, len(partners))
    for a in range(arrays):
        for stage in range(len(bits)):
            outgoing(a, 1 << stage).start()
    for a in range(arrays):
        own(a).start()
    for k in range(1, data_count):
        for a in range(arrays):
            incoming(a, k).wait_recv()
            for stage in range(k.bit_length(), len(bits)):
                outgoing(a, k + (1 << stage)).start()
            passed(a, k).start()
    for a in range(arrays):
        own(a).wait()
        for k in range(1, data_count):
            pass_in(a, k).wait_recv()
            passed(a, k).wait_send()
            outgoing(a, k).wait_send()


def gather_rows(shards):
    data_count = lax.axis_size("dp")
    anywhere = pl.BlockSpec(memory_space=pl.ANY)
    shape = (len(shards), data_count)
    return pl.pallas_call(
        functools.partial(gather_kernel, data_count),
        out_shape=[
            jax.ShapeDtypeStruct((shard.shape[0] * data_count,) + shard.shape[1:], shard.dtype)
            for shard in shards
        ],
        in_specs=[anywhere] * len(shards),
        out_specs=[anywhere] * len(shards),
        scratch_shapes=[pltpu.SemaphoreType.DMA(shape)] * 4
        + [pltpu.SemaphoreType.DMA((len(shards),))],
        compiler_params=pltpu.CompilerParams(collective_id=0, has_side_effects=True),
        name="gather_weights",
    )(*shards)


def carried_in(log_total, state, expand, backward, beside=None):
    mine = lax.axis_index("ctx")
    core = mine % 2
    half = state.shape[0] // 2

    def is_after(bit):
        is_high = (mine & bit) != 0
        return jnp.logical_not(is_high) if backward else is_high

    partner = swap_ctx(state, 1)
    partner_log = swap_ctx(log_total, 1)
    late = is_after(1)
    late_log = jnp.where(late, log_total, partner_log)
    own_half = lax.dynamic_slice_in_dim(state, core * half, half, 0)
    partner_half = lax.dynamic_slice_in_dim(partner, core * half, half, 0)
    early_half = jnp.where(late, partner_half, own_half)
    late_half = jnp.where(late, own_half, partner_half)
    total = jnp.exp(expand(late_log)) * early_half + late_half
    total_log = log_total + partner_log
    prefix_log, prefix = jnp.zeros_like(log_total), jnp.zeros_like(total)
    extra = None
    for bit in bits_of(lax.axis_size("ctx"))[1:]:
        got = swap_ctx(total, bit)
        if beside is not None and 2 * bit == lax.axis_size("ctx"):
            extra, got = lax.optimization_barrier((beside(total), got))
        got_log = swap_ctx(total_log, bit)
        after = is_after(bit)
        prefix = jnp.where(after, jnp.exp(expand(prefix_log)) * got + prefix, prefix)
        prefix_log = jnp.where(after, prefix_log + got_log, prefix_log)
        joined_mine = jnp.exp(expand(total_log)) * got + total
        total = jnp.where(after, joined_mine, jnp.exp(expand(got_log)) * total + got)
        total_log = total_log + got_log
    other = swap_ctx(prefix, 1)
    first = jnp.where(core == 0, prefix, other)
    second = jnp.where(core == 0, other, prefix)
    whole_prefix = jnp.concatenate([first, second], axis=0)
    joined = jnp.where(late, jnp.exp(expand(partner_log)) * whole_prefix + partner, whole_prefix)
    return (joined, extra)


def fdot(left, right, dims, precision=HIGH):
    return lax.dot_general(left, right, dims, precision=precision, preferred_element_type=F32)


def per_device(
    tokens,
    grad_output,
    session_ids,
    session_table,
    norm_gain,
    input_weight,
    step_weight,
    head_params,
    gate_gain,
    output_weight,
):
    data_count, context_count = lax.axis_size("dp"), lax.axis_size("ctx")
    num_seqs, bins, model_width = tokens.shape
    assert num_seqs == 1
    width = output_weight.shape[0] * data_count
    num_heads = step_weight.shape[1]
    head_width = width // num_heads
    state_width = (input_weight.shape[1] - 2 * width) // 2
    sessions = session_table.shape[0]
    chunks = bins // CHUNK
    grad_scale = 1.0 / math.sqrt(bins * data_count * context_count)
    tokens, grad_output = tokens[0], grad_output[0]

    session_low = jnp.broadcast_to(session_ids.astype(BF16)[None, :], (step_weight.shape[0], 1))
    side = jnp.concatenate(
        [step_weight, norm_gain[:, None], gate_gain[:, None], session_low], axis=1
    )
    side = jnp.pad(side, ((0, 0), (0, -side.shape[1] % 128)))
    input_full, side_full, output_full = gather_rows([input_weight, side, output_weight])
    step_full = side_full[:, :num_heads]
    norm_full = side_full[:, num_heads].astype(F32)[None, :]
    gate_full = side_full[:, num_heads + 1].astype(F32)[None, :]
    all_sessions = side_full[:: step_weight.shape[0], num_heads + 2].astype(jnp.int32)

    table_row = lax.dynamic_slice_in_dim(session_table, session_ids[0], 1, 0).astype(F32)
    layer_in = tokens.astype(F32) + table_row
    in_scale = lax.rsqrt(jnp.mean(layer_in * layer_in, axis=-1, keepdims=True) + epsilon)
    normed = layer_in * in_scale
    norm_act = (normed * norm_full).astype(BF16)
    projected = fdot(norm_act, input_full, NN, None)
    step_raw = fdot(norm_act, step_full, NN, None)
    gate_pre = projected[:, :width]
    value_raw = projected[:, width : 2 * width]
    in_map = projected[:, 2 * width : 2 * width + state_width]
    out_map = projected[:, 2 * width + state_width :]
    in_t, out_t = in_map.T, out_map.T

    step_in = step_raw + head_params[0][None, :]
    step_size = jax.nn.softplus(step_in)
    rate = jnp.exp(head_params[1])[None, :]
    log_rate = -rate * step_size
    position = jnp.arange(bins)
    lower = position[:, None] >= position[None, :]
    same = (position[:, None] // CHUNK) == (position[None, :] // CHUNK)
    lower_all = lower.astype(F32)
    lower_chunk = (lower & same).astype(F32)
    log_local = fdot(lower_chunk, log_rate, NN, HIGHEST)
    log_row = fdot(log_rate, lower_chunk, (((0,), (1,)), ((), ())), HIGHEST)
    log_decay = fdot(lower_all, log_rate, NN, HIGHEST)
    log_total = jnp.sum(log_rate, axis=0)
    hot = (jnp.arange(num_heads)[:, None] == jnp.arange(width)[None, :] // head_width).astype(F32)

    def expand(value):
        return jnp.repeat(value, head_width, axis=-1)[None, :]

    def widen(value):
        return fdot(value, hot, NN, HIGHEST)

    def per_head(value):
        return fdot(value, hot, NT, HIGH)

    step_wide, local_wide, decay_wide = (widen(step_size), widen(log_local), widen(log_decay))
    log_row = log_row.reshape(width // PAIR, 2, bins)
    value_sig = jax.nn.sigmoid(value_raw)
    activated = value_raw * value_sig
    scaled_in = step_wide * activated
    total_wide = expand(log_total)
    tail_wide = jnp.exp(total_wide - decay_wide)
    tail_scaled = tail_wide * scaled_in
    state_local = fdot(in_map, tail_scaled, TN)

    def beside(ready):
        local, ready = lax.optimization_barrier((local_wide, ready))
        return core_forward(value_raw, step_wide, local, log_row, in_map, in_t, out_map)

    state_in, result_local = carried_in(log_total, state_local, expand, False, beside)
    grad_mixed = fdot(grad_output, output_full, NT, None)
    skip_wide = expand(head_params[2])
    decay_in = jnp.exp(decay_wide)
    result = result_local + decay_in * fdot(out_map, state_in, NN)
    ssd_out = result + skip_wide * activated
    gate_sig = jax.nn.sigmoid(gate_pre)
    gate_act = gate_pre * gate_sig
    gated = ssd_out * gate_act
    gate_scale = lax.rsqrt(jnp.mean(gated * gated, axis=-1, keepdims=True) + epsilon)
    gated_norm = gated * gate_scale
    mixed_out = (gated_norm * gate_full).astype(BF16)
    term_gate = jnp.sum(grad_mixed * gated_norm, axis=0) * grad_scale
    grad_gnorm = grad_mixed * gate_full
    grad_gated = gate_scale * (
        grad_gnorm - gated_norm * jnp.mean(grad_gnorm * gated_norm, axis=-1, keepdims=True)
    )
    grad_ssd = grad_gated * gate_act
    grad_gate = grad_gated * ssd_out * gate_sig * (1.0 + gate_pre * (1.0 - gate_sig))

    adjoint_local = fdot(out_map, decay_in * grad_ssd, TN)
    grad_gate_low = grad_gate.astype(BF16)
    term_output = fdot(mixed_out, grad_output, TN, None) * grad_scale
    term_gate_in = fdot(norm_act, grad_gate_low, TN, None) * grad_scale
    early = scatter_steps([term_output, term_gate_in])
    first = next(early)

    def beside_adjoint(ready):
        local, ready, message = lax.optimization_barrier((local_wide, ready, first))
        outputs = core_backward(
            value_raw,
            step_wide,
            local,
            log_row,
            in_map,
            in_t,
            out_map,
            out_t,
            grad_ssd,
            state_in,
        )
        return lax.optimization_barrier((outputs, early.send(message)))

    adjoint_out, (outputs, got) = carried_in(
        log_total, adjoint_local, expand, True, beside_adjoint
    )
    dx_local, din_local, dout = outputs
    message = early.send(got)
    dx_local, message = lax.optimization_barrier((dx_local, message))
    got = early.send(message)
    grad_scaled = dx_local + tail_wide * fdot(in_map, adjoint_out, NN)
    grad_in_map = din_local + fdot(tail_scaled, adjoint_out, NT)
    state_end = jnp.exp(total_wide) * state_in + state_local
    end_term = per_head(jnp.sum(state_end * adjoint_out, axis=0, keepdims=True))
    pull_step = per_head(activated * grad_scaled)
    pull_log = per_head(grad_ssd * result) - step_size * pull_step
    grad_rate = fdot(lower_all, pull_log, TN, HIGHEST) + end_term
    grad_step_size = pull_step - rate * grad_rate
    grad_step_raw = grad_step_size * jax.nn.sigmoid(step_in)
    grad_heads = jnp.stack(
        [
            jnp.sum(grad_step_raw, axis=0),
            jnp.sum(grad_rate * log_rate, axis=0),
            per_head(jnp.sum(grad_ssd * activated, axis=0, keepdims=True))[0],
        ]
    )
    grad_active = step_wide * grad_scaled + skip_wide * grad_ssd
    grad_value = grad_active * value_sig * (1.0 + value_raw * (1.0 - value_sig))
    grad_late = jnp.concatenate(
        [grad_value.astype(BF16), grad_in_map.astype(BF16), dout.astype(BF16)], axis=1
    )
    grad_step_low = grad_step_raw.astype(BF16)
    grad_late, got = lax.optimization_barrier((grad_late, got))
    message = early.send(got)
    grad_late, message = lax.optimization_barrier((grad_late, message))
    got = early.send(message)
    term_late = fdot(norm_act, grad_late, TN, None) * grad_scale
    grad_act = (
        fdot(grad_gate_low, input_full[:, :width], NT, None)
        + fdot(grad_late, input_full[:, width:], NT, None)
        + fdot(grad_step_low, step_full, NT, None)
    )
    term_step = fdot(norm_act, grad_step_low, TN, None) * grad_scale
    term_norm = jnp.sum(grad_act * normed, axis=0) * grad_scale
    grad_normed = grad_act * norm_full
    grad_input = in_scale * (
        grad_normed - normed * jnp.mean(grad_normed * normed, axis=-1, keepdims=True)
    )
    term_table = jnp.sum(grad_input, axis=0) * grad_scale

    rows = model_width // (data_count * context_count)
    head_columns = -(-grad_heads.size // rows)
    heads = jnp.zeros((head_columns * rows,), F32).at[: grad_heads.size].set(grad_heads.ravel())
    heads = jnp.tile(heads.reshape(head_columns, rows).T * grad_scale, (model_width // rows, 1))
    slot = (jnp.arange(data_count) == lax.axis_index("dp")).astype(F32)
    rider = jnp.concatenate(
        [
            term_norm[:, None],
            term_gate[:, None],
            term_step,
            heads,
            term_table[:, None] * slot[None, :],
        ],
        axis=1,
    )
    late_steps = scatter_steps([term_late], [rider])
    late, rider = finish(late_steps, next(late_steps))
    output_grad, early_gate = finish(early, got)
    split_at = 2 + num_heads
    heads = rider[:, split_at : split_at + head_columns].T.ravel()[: grad_heads.size]
    session_hot = (all_sessions[:, None] == jnp.arange(sessions)[None, :]).astype(F32)
    table_grad = fdot(session_hot, rider[:, split_at + head_columns :], (((0,), (1,)), ((), ())), HIGHEST)
    return (
        grad_input.astype(BF16)[None],
        rider[:, 0],
        jnp.concatenate([early_gate, late], axis=1),
        rider[:, 2:split_at],
        heads.reshape(grad_heads.shape),
        rider[:, 1],
        output_grad,
        table_grad,
    )


def solution(mesh):
    placed = (
        P("dp", "ctx", None),
        P("dp", "ctx", None),
        P("dp"),
        P(),
        P("dp"),
        P("dp", None),
        P("dp", None),
        P(),
        P("dp"),
        P("dp", None),
    )
    return jax.shard_map(
        per_device,
        mesh=mesh,
        in_specs=placed,
        out_specs=(
            P("dp", "ctx", None),
            P(("dp", "ctx")),
            P(("dp", "ctx"), None),
            P(("dp", "ctx"), None),
            P(),
            P(("dp", "ctx")),
            P(("dp", "ctx"), None),
            P(None, ("dp", "ctx")),
        ),
        check_vma=False,
    )
```
